32 devices in a mesh: groups: 2 (over y), seq: 4 (over z), head: 2 (over x), hsub: 2 (over core).
Axes of the slice: x: 2, y: 2, z: 4, core: 2. Of those that a mesh axis runs over, the one named last changes fastest.
Arguments:
- token_values: bfloat16 [16384, 2048], P(('groups', 'seq'), ('head', 'hsub')), parts along dimension 0, may hold values from -0.125 to 0.125
- key_proj: bfloat16 [16384, 128], P(('groups', 'seq')), parts along dimension 0, may hold values from -0.5 to 0.5
- query_proj: bfloat16 [16384, 128], P(('groups', 'seq')), parts along dimension 0, may hold values from -0.5 to 0.5
- log_decay: float32 [32, 16384], P(('head', 'hsub'), ('groups', 'seq')), parts along dimension 1, may hold values from 0 to 2, as said below
- out_grad: bfloat16 [16384, 2048], P(('groups', 'seq'), ('head', 'hsub')), parts along dimension 0, may hold values from -6 to 6
Outputs:
- value_grad: bfloat16 [16384, 2048], P(('groups', 'seq'), ('head', 'hsub')), parts along dimension 0
- key_grad: float32 [16384, 128], P(('groups', 'seq', 'head', 'hsub')), parts along dimension 0
- query_grad: float32 [16384, 128], P(('groups', 'seq', 'head', 'hsub')), parts along dimension 0
The draws below stay inside these ranges and needn't reach their ends.
There are 2 independent parts, one for each index of `groups`. The reference program is written for one: setup_inputs(seed, part) draws one part's arguments, and reference() takes and returns one part's arrays. A program takes and returns all parts, laid end to end along the dimension named above; each array names one. Nothing has to cross between parts.
Inputs may be any that keep to these rules, and one draw needn't show every extreme that they name: log_decay is positive.
All inputs are finite; a program needn't handle non-finite values.
Results may differ from the reference program's by a relative error of at most 0.0057.
Values sent between devices are 32-bit elements; how exact they have to be, the bound alone decides.
A program may use at most 128 MiB of HBM per device.

```python
import math
import jax
import jax.numpy as jnp
from jax import lax

HEADS = 32
HEAD_DIM = 64
STATE = 128
BLOCK = 128
TOK_DEV = 2048
TOKENS = 8192


def draw_log_decay(key, part):
    streams = jax.random.split(key, 8)
    fast_rate = jnp.exp(jax.random.uniform(streams[1], (HEADS,), minval=math.log(1.0 / 50.0), maxval=math.log(1.0 / 30.0)))
    faster = jax.random.uniform(streams[0], (HEADS,)) < 0.3
    other_rate = jnp.exp(jax.random.uniform(streams[7], (HEADS,), minval=math.log(1.5), maxval=math.log(5.0))) / TOK_DEV
    base = jnp.where(faster, fast_rate, other_rate)
    blocks = TOKENS // TOK_DEV
    device_multiplier = jnp.exp(jax.random.uniform(streams[3], (HEADS, blocks, 1), minval=math.log(0.5), maxval=math.log(2.0)))
    roughness = jax.random.uniform(streams[4], (HEADS, blocks, TOK_DEV), minval=0.5, maxval=1.5)
    speed_entries = (base[:, None, None] * device_multiplier * roughness).reshape(HEADS, TOKENS)
    location_numbers = jax.random.randint(streams[5], (HEADS, 2, 1), 0, TOKENS)
    quantity_entries = jax.random.uniform(streams[6], (HEADS, 2, 1), minval=0.22, maxval=0.69)
    element_offset = jnp.arange(TOKENS)[None, None, :]
    cluster_sets = jnp.sum(jnp.where(element_offset == location_numbers, quantity_entries, 0.0), axis=1)
    return (speed_entries + cluster_sets).astype(jnp.float32)


def shard_levels(rng, shape, cuts, low, top_value):
    gain, own = 1.0, jax.random.fold_in(rng, 6)
    for axis_at, blocks in cuts:
        heights = jnp.exp(jax.random.uniform(jax.random.fold_in(own, axis_at), (blocks,), jnp.float32, low / len(cuts), top_value / len(cuts)))
        gain = gain * jnp.repeat(heights, shape[axis_at] // blocks).reshape([-1 if axis == axis_at else 1 for axis in range(len(shape))])
    return gain


def centred(key, extent, deviation, limit, cuts=(), kind=jnp.bfloat16):
    values = deviation * jax.random.normal(key, extent, jnp.float32)
    if cuts:
        values = values * shard_levels(key, extent, cuts, -0.22, 0.18)
    return jnp.clip(values, -limit, limit).astype(kind)


def setup_inputs(seed: int = 0, part: int = 0) -> dict:
    seeds = jax.random.split(jax.random.key(seed), 6)
    part_keys = jax.random.split(jax.random.fold_in(seeds[5], part), 6)
    return {
        "token_values": centred(part_keys[0], (TOKENS, HEADS * HEAD_DIM), ((STATE * TOKENS) ** 0.25 / ((HEADS * HEAD_DIM) ** 0.5 * TOKENS ** 0.5)), 0.125, ((0, 4), (1, 4))),
        "key_proj": centred(part_keys[1], (TOKENS, STATE), (1.0 / (STATE * TOKENS) ** 0.25), 0.5, ((0, 4),)),
        "query_proj": centred(part_keys[2], (TOKENS, STATE), (1.0 / (STATE * TOKENS) ** 0.25), 0.5, ((0, 4),)),
        "log_decay": draw_log_decay(jax.random.fold_in(jax.random.fold_in(seeds[5], part), 71), part),
        "out_grad": centred(part_keys[4], (TOKENS, HEADS * HEAD_DIM), 1.0, 6.0, ((0, 4), (1, 4))),
    }


def rounded(array):
    return lax.optimization_barrier(array.astype(jnp.bfloat16)).astype(jnp.float32)


def advance(carry, pieces):
    return pieces[0] * carry + pieces[1], carry


def reference(token_values, key_proj, query_proj, log_decay, out_grad):
    highest = lax.Precision.HIGHEST
    count = TOKENS // BLOCK
    key_rows = key_proj.astype(jnp.float32).reshape(count, BLOCK, STATE)
    query_rows = query_proj.astype(jnp.float32).reshape(count, BLOCK, STATE)
    scores = jnp.einsum('cin,cjn->cij', query_rows, key_rows, precision=highest)
    within_all = jnp.cumsum(log_decay.reshape(HEADS, count, BLOCK), axis=2)
    values_all = token_values.astype(jnp.float32).reshape(count, BLOCK, HEADS, HEAD_DIM)
    grads_all = out_grad.astype(jnp.float32).reshape(count, BLOCK, HEADS, HEAD_DIM)
    positions = jnp.arange(BLOCK)
    causal = positions[:, None] >= positions[None, :]
    zero_state = jnp.zeros((STATE, HEAD_DIM), jnp.float32)

    def one_head(sums, head):
        values = lax.dynamic_index_in_dim(values_all, head, 2, keepdims=False)
        grads = lax.dynamic_index_in_dim(grads_all, head, 2, keepdims=False)
        within = lax.dynamic_index_in_dim(within_all, head, 0, keepdims=False)
        block_last = within[:, -1]
        inside = within[:, :, None] - within[:, None, :]
        decay_mask = jnp.exp(-jnp.where(causal[None], inside, jnp.inf))
        mixed = rounded(decay_mask * scores)
        pairs = jnp.einsum('cip,cjp->cij', grads, values, precision=highest)
        pair_mask = rounded(decay_mask * pairs)
        tail_weight = jnp.exp(within - block_last[:, None])
        lead_weight = jnp.exp(-within)
        tail_keys = rounded(tail_weight[..., None] * key_rows)
        lead_queries = rounded(lead_weight[..., None] * query_rows)
        block_states = jnp.einsum('cjn,cjp->cnp', tail_keys, values, precision=highest)
        block_adjoints = jnp.einsum('cin,cip->cnp', lead_queries, grads, precision=highest)
        decays = jnp.exp(-block_last)
        unused, entering = lax.scan(advance, zero_state, (decays, block_states))
        unused_too, after = lax.scan(advance, zero_state, (decays, block_adjoints), reverse=True)
        entering_low = rounded(entering)
        after_low = rounded(after)
        value_part = jnp.einsum('cij,cip->cjp', mixed, grads, precision=highest)
        value_part = value_part + tail_weight[..., None] * jnp.einsum('cjn,cnp->cjp', key_rows, after_low, precision=highest)
        key_part = jnp.einsum('cij,cin->cjn', pair_mask, query_rows, precision=highest)
        key_part = key_part + tail_weight[..., None] * jnp.einsum('cjp,cnp->cjn', values, after_low, precision=highest)
        query_part = jnp.einsum('cij,cjn->cin', pair_mask, key_rows, precision=highest)
        query_part = query_part + lead_weight[..., None] * jnp.einsum('cip,cnp->cin', grads, entering_low, precision=highest)
        return (sums[0] + key_part, sums[1] + query_part), value_part.reshape(TOKENS, HEAD_DIM)

    start = (jnp.zeros((count, BLOCK, STATE), jnp.float32), jnp.zeros((count, BLOCK, STATE), jnp.float32))
    sums, per_head = lax.scan(one_head, start, jnp.arange(HEADS, dtype=jnp.int32))
    value_grad = jnp.transpose(per_head, (1, 0, 2)).reshape(TOKENS, HEADS * HEAD_DIM).astype(jnp.bfloat16)
    return value_grad, sums[0].reshape(TOKENS, STATE), sums[1].reshape(TOKENS, STATE)
```

```python
import functools
import jax
import jax.numpy as jnp
from jax import lax
from jax.experimental import pallas as pl
from jax.experimental.pallas import tpu as pltpu
from jax.sharding import PartitionSpec as P

BLOCK = 128
LANES = 128
WIDE = jnp.float32
LOW = jnp.bfloat16
MESH = pl.DeviceIdType.MESH


def product(a, b, over):
    return lax.dot_general(a, b, (((over[0],), (over[1],)), ((), ())), preferred_element_type=WIDE)


def kernel(
    sizes, heads,
    v_ref, k_ref, q_ref, ld_ref, g_ref,
    val_ref, kg_ref, qg_ref,
    within, wst, tv, lg, tw, states, adjoints, decays, ent, aft,
    own_f, own_b, total, f_in, f_out, b_in, b_out, acc, buf_a, buf_b,
    f_send, f_recv, b_send, b_recv, a_send, a_recv, x_send, x_recv,
):
    n_seq, n_head, n_sub = sizes
    length, cols = v_ref.shape
    state = k_ref.shape[1]
    channels = cols // heads
    count = length // BLOCK
    chunks = cols // LANES
    per = LANES // channels
    pad = wst.shape[1] // 2
    rows_out = length // (n_head * n_sub)
    blocks_out = rows_out // BLOCK
    s = lax.axis_index("seq")
    x = lax.axis_index("head")
    u = lax.axis_index("hsub")

    barrier = pltpu.get_barrier_semaphore()

    @pl.when(s > 0)
    def _():
        pl.semaphore_signal(barrier, inc=1, device_id={"seq": s - 1}, device_id_type=MESH)

    @pl.when(s < n_seq - 1)
    def _():
        pl.semaphore_signal(barrier, inc=1, device_id={"seq": s + 1}, device_id_type=MESH)

    for e in range(1, n_sub):
        pl.semaphore_signal(
            barrier, inc=1, device_id={"hsub": lax.rem(u + e, n_sub)}, device_id_type=MESH
        )
    for d in range(1, n_head):
        pl.semaphore_signal(
            barrier, inc=1, device_id={"head": lax.rem(x + d, n_head)}, device_id_type=MESH
        )

    def rows_of(c):
        return pl.ds(pl.multiple_of(c * BLOCK, BLOCK), BLOCK)

    row_at = lax.broadcasted_iota(jnp.int32, (BLOCK, BLOCK), 0)
    col_at = lax.broadcasted_iota(jnp.int32, (BLOCK, BLOCK), 1)
    upper = row_at <= col_at
    tri = jnp.where(upper, 1.0, 0.0).astype(WIDE)
    e_row = lax.broadcasted_iota(jnp.int32, (2 * pad, cols), 0)
    e_col = lax.broadcasted_iota(jnp.int32, (2 * pad, cols), 1)
    spread = jnp.where(lax.rem(e_row, pad) == e_col // channels, 1.0, 0.0).astype(LOW)
    lane_head = lax.broadcasted_iota(jnp.int32, (BLOCK, LANES), 1) // channels

    wst[...] = jnp.zeros_like(wst)
    own_f[...] = jnp.zeros_like(own_f)
    own_b[...] = jnp.zeros_like(own_b)
    total[...] = jnp.ones_like(total)

    def expand(slot, w):
        high = w.astype(LOW).astype(WIDE)
        wst[slot, 0:heads, :] = high
        wst[slot, pad:pad + heads, :] = w - high
        return product(wst[slot].astype(LOW), spread, (0, 0))

    def block_sums(c, _):
        rows = rows_of(c)
        w = lax.dot_general(
            ld_ref[:, rows], tri, (((1,), (0,)), ((), ())),
            precision=lax.Precision.HIGHEST, preferred_element_type=WIDE,
        )
        within[c] = w
        tail = expand(0, jnp.exp(w - w[:, BLOCK - 1:BLOCK]))
        lead = expand(1, jnp.exp(-w))
        tw[rows, :] = tail
        scaled_v = (tail * v_ref[rows, :].astype(WIDE)).astype(LOW)
        scaled_g = (lead * g_ref[rows, :].astype(WIDE)).astype(LOW)
        tv[rows, :] = scaled_v
        lg[rows, :] = scaled_g
        b = product(k_ref[rows, :], scaled_v, (0, 0))
        a = product(q_ref[rows, :], scaled_g, (0, 0))
        states[c] = b
        adjoints[c] = a
        for k in range(chunks):
            part = slice(k * LANES, (k + 1) * LANES)
            decay = lead[BLOCK - 1:BLOCK, part]
            decays[c, k] = decay
            own_f[k] = decay * own_f[k] + b[:, part]
            own_b[k] = own_b[k] + total[k] * a[:, part]
            total[k] = total[k] * decay
        return 0

    lax.fori_loop(0, count, block_sums, 0)

    def f_copy(k):
        return pltpu.make_async_remote_copy(
            src_ref=f_out.at[k], dst_ref=f_in.at[k], send_sem=f_send.at[k], recv_sem=f_recv.at[k],
            device_id={"seq": lax.rem(s + 1, n_seq)}, device_id_type=MESH,
        )

    def b_copy(k):
        return pltpu.make_async_remote_copy(
            src_ref=b_out.at[k], dst_ref=b_in.at[k], send_sem=b_send.at[k], recv_sem=b_recv.at[k],
            device_id={"seq": lax.rem(s + n_seq - 1, n_seq)}, device_id_type=MESH,
        )

    near = jnp.where(s > 0, 1, 0) + jnp.where(s < n_seq - 1, 1, 0) + (n_sub - 1) + (n_head - 1)
    pl.semaphore_wait(barrier, near)

    @pl.when(s == 0)
    def _():
        f_in[...] = jnp.zeros_like(f_in)

    @pl.when(s == n_seq - 1)
    def _():
        b_in[...] = jnp.zeros_like(b_in)

    if n_seq > 1:
        @pl.when(s == 0)
        def _():
            for k in range(chunks):
                f_out[k] = own_f[k]
                f_copy(k).start()

        @pl.when(s == n_seq - 1)
        def _():
            for k in range(chunks):
                b_out[k] = own_b[k]
                b_copy(k).start()

    f_at = jnp.minimum(3 * s, count - chunks)
    b_at = jnp.minimum(3 * (n_seq - 1 - s), count - chunks)

    def mask(wt, wt_t, h):
        return jnp.exp(jnp.minimum(wt_t[:, h:h + 1] - wt[h:h + 1, :], 0.0))

    def pair_work(c, _):
        rows = rows_of(c)
        wt = within[c]
        wt_t = wt.T
        pair_sum = jnp.zeros((BLOCK, BLOCK), WIDE)
        for p in range(chunks):
            part = slice(p * LANES, (p + 1) * LANES)
            v2 = v_ref[rows, part]
            g2 = g_ref[rows, part]
            stack = jnp.concatenate(
                [jnp.where(lane_head == r, v2, jnp.zeros_like(v2)) for r in range(per)], axis=0
            )
            pairs = product(stack, g2, (1, 1))
            for r in range(per):
                pair_sum += mask(wt, wt_t, p * per + r) * pairs[r * BLOCK:(r + 1) * BLOCK, :]
        pair_low = jnp.where(upper, pair_sum, 0.0).astype(LOW)
        acc[1, rows, :] = product(pair_low, q_ref[rows, :], (1, 0))
        acc[0, rows, :] = product(pair_low, k_ref[rows, :], (0, 0))

        if n_seq > 1:
            kf = c - f_at

            @pl.when((s > 0) & (kf >= 0) & (kf < chunks))
            def _():
                f_copy(kf).wait_recv()

                @pl.when(s < n_seq - 1)
                def _():
                    f_out[kf] = total[kf] * f_in[kf] + own_f[kf]
                    f_copy(kf).start()

            kb = c - b_at

            @pl.when((s < n_seq - 1) & (kb >= 0) & (kb < chunks))
            def _():
                b_copy(kb).wait_recv()

                @pl.when(s > 0)
                def _():
                    b_out[kb] = total[kb] * b_in[kb] + own_b[kb]
                    b_copy(kb).start()
        return 0

    lax.fori_loop(0, count, pair_work, 0)

    for k in range(chunks):
        part = slice(k * LANES, (k + 1) * LANES)

        def step(c, carry, k=k, part=part):
            f, b = carry
            e = count - 1 - c
            ent[c, :, part] = f.astype(LOW)
            aft[e, :, part] = b.astype(LOW)
            return (decays[c, k] * f + states[c, :, part], decays[e, k] * b + adjoints[e, :, part])

        lax.fori_loop(0, count, step, (f_in[k], b_in[k]))

    def carried(which, base):
        def one(t, _):
            c = base * blocks_out + t
            rows = rows_of(c)
            if which == 0:
                acc[0, rows, :] += product(lg[rows, :], ent[c], (1, 1))
            else:
                acc[1, rows, :] += product(tv[rows, :], aft[c], (1, 1))
            return 0

        lax.fori_loop(0, blocks_out, one, 0)

    def piece(base):
        return pl.ds(pl.multiple_of(base * rows_out, rows_out), rows_out)

    def a_copy(d, e, which):
        far = lax.rem(u + e, n_sub)
        base = lax.rem(x + d, n_head) * n_sub + far
        return pltpu.make_async_remote_copy(
            src_ref=acc.at[which, piece(base)], dst_ref=buf_a.at[d, e - 1, which],
            send_sem=a_send.at[d, e - 1, which], recv_sem=a_recv.at[d, e - 1, which],
            device_id={"hsub": far}, device_id_type=MESH,
        )

    def x_copy(d, which):
        far = lax.rem(x + d, n_head)
        return pltpu.make_async_remote_copy(
            src_ref=acc.at[which, piece(far * n_sub + u)], dst_ref=buf_b.at[d - 1, which],
            send_sem=x_send.at[d - 1, which], recv_sem=x_recv.at[d - 1, which],
            device_id={"head": far}, device_id_type=MESH,
        )

    order = list(range(1, n_head)) + [0]
    for d in order:
        far = lax.rem(x + d, n_head)
        for which in range(2):
            for e in range(1, n_sub):
                carried(which, far * n_sub + lax.rem(u + e, n_sub))
                a_copy(d, e, which).start()
        for which in range(2):
            carried(which, far * n_sub + u)
        for which in range(2):
            own = piece(far * n_sub + u)
            for e in range(1, n_sub):
                a_copy(d, e, which).wait_recv()
                acc[which, own, :] += buf_a[d, e - 1, which]
            if d > 0:
                x_copy(d, which).start()

    def value_work(c, _):
        rows = rows_of(c)
        wt = within[c]
        wt_t = wt.T
        key = k_ref[rows, :]
        scores = jnp.where(upper, product(key, q_ref[rows, :], (1, 1)), 0.0)
        back = product(key, aft[c], (1, 0)) * tw[rows, :]
        for p in range(chunks):
            part = slice(p * LANES, (p + 1) * LANES)
            g2 = g_ref[rows, part]
            mixed = jnp.concatenate(
                [(mask(wt, wt_t, p * per + r) * scores).astype(LOW) for r in range(per)], axis=1
            )
            stack = jnp.concatenate(
                [jnp.where(lane_head == r, g2, jnp.zeros_like(g2)) for r in range(per)], axis=0
            )
            val_ref[rows, part] = (product(mixed, stack, (1, 0)) + back[:, part]).astype(LOW)
        return 0

    lax.fori_loop(0, count, value_work, 0)

    mine = piece(x * n_sub + u)
    for which, out in ((0, qg_ref), (1, kg_ref)):
        result = acc[which, mine, :]
        for d in range(1, n_head):
            x_copy(d, which).wait_recv()
            result = result + buf_b[d - 1, which]
        out[...] = result

    for which in range(2):
        for d in range(n_head):
            for e in range(1, n_sub):
                a_copy(d, e, which).wait_send()
        for d in range(1, n_head):
            x_copy(d, which).wait_send()

    @pl.when(s < n_seq - 1)
    def _():
        for k in range(chunks):
            f_copy(k).wait_send()

    @pl.when(s > 0)
    def _():
        for k in range(chunks):
            b_copy(k).wait_send()


def local(sizes, token_values, key_proj, query_proj, log_decay, out_grad):
    n_seq, n_head, n_sub = sizes
    length, cols = token_values.shape
    heads = log_decay.shape[0]
    state = key_proj.shape[1]
    count = length // BLOCK
    chunks = cols // LANES
    pad = (heads + 7) // 8 * 8
    rows_out = length // (n_head * n_sub)
    vmem = pl.BlockSpec(memory_space=pltpu.VMEM)
    dma = pltpu.SemaphoreType.DMA
    subs = max(n_sub - 1, 1)
    fars = max(n_head - 1, 1)
    square = pltpu.VMEM((chunks, state, LANES), WIDE)
    value_grad, key_grad, query_grad = pl.pallas_call(
        functools.partial(kernel, sizes, heads),
        out_shape=(
            jax.ShapeDtypeStruct((length, cols), LOW),
            jax.ShapeDtypeStruct((rows_out, state), WIDE),
            jax.ShapeDtypeStruct((rows_out, state), WIDE),
        ),
        in_specs=[vmem] * 5,
        out_specs=(vmem, vmem, vmem),
        scratch_shapes=[
            pltpu.VMEM((count, heads, BLOCK), WIDE),
            pltpu.VMEM((2, 2 * pad, BLOCK), WIDE),
            pltpu.VMEM((length, cols), LOW),
            pltpu.VMEM((length, cols), LOW),
            pltpu.VMEM((length, cols), WIDE),
            pltpu.VMEM((count, state, cols), WIDE),
            pltpu.VMEM((count, state, cols), WIDE),
            pltpu.VMEM((count, chunks, 1, LANES), WIDE),
            pltpu.VMEM((count, state, cols), LOW),
            pltpu.VMEM((count, state, cols), LOW),
            square, square, pltpu.VMEM((chunks, 1, LANES), WIDE),
            square, square, square, square,
            pltpu.VMEM((2, length, state), WIDE),
            pltpu.VMEM((n_head, subs, 2, rows_out, state), WIDE),
            pltpu.VMEM((fars, 2, rows_out, state), WIDE),
            dma((chunks,)), dma((chunks,)), dma((chunks,)), dma((chunks,)),
            dma((n_head, subs, 2)), dma((n_head, subs, 2)),
            dma((fars, 2)), dma((fars, 2)),
        ],
        compiler_params=pltpu.CompilerParams(
            collective_id=0, has_side_effects=True, vmem_limit_bytes=56 * 1024 * 1024
        ),
    )(token_values, key_proj, query_proj, log_decay, out_grad)
    return value_grad, key_grad, query_grad


def solution(mesh):
    sizes = (mesh.shape["seq"], mesh.shape["head"], mesh.shape["hsub"])
    placed = (
        P(("groups", "seq"), ("head", "hsub")),
        P(("groups", "seq"), None),
        P(("groups", "seq"), None),
        P(("head", "hsub"), ("groups", "seq")),
        P(("groups", "seq"), ("head", "hsub")),
    )
    return jax.shard_map(
        functools.partial(local, sizes),
        mesh=mesh,
        in_specs=placed,
        out_specs=(
            P(("groups", "seq"), ("head", "hsub")),
            P(("groups", "seq", "head", "hsub"), None),
            P(("groups", "seq", "head", "hsub"), None),
        ),
        check_vma=False,
    )
```

```python
import functools
import jax
import jax.numpy as jnp
from jax import lax
from jax.experimental import pallas as pl
from jax.experimental.pallas import tpu as pltpu
from jax.sharding import PartitionSpec as P

BLOCK = 128
LANES = 128
WIDE = jnp.float32
LOW = jnp.bfloat16
MESH = pl.DeviceIdType.MESH
UNROLL = 2
DEEP = 4


def product(a, b, over):
    return lax.dot_general(a, b, (((over[0],), (over[1],)), ((), ())), preferred_element_type=WIDE)


def kernel(
    sizes, heads,
    v_ref, k_ref, q_ref, ld_ref, g_ref,
    val_ref, kg_ref, qg_ref,
    within, wst, stacked, tv, lg, tw, states, adjoints, decays, ent, aft,
    own_f, own_b, total, f_in, f_out, b_in, b_out, acc, buf_a, buf_b,
    f_send, f_recv, b_send, b_recv, a_send, a_recv, x_send, x_recv,
):
    n_seq, n_head, n_sub = sizes
    length, cols = v_ref.shape
    state = k_ref.shape[1]
    channels = cols // heads
    count = length // BLOCK
    chunks = cols // LANES
    per = LANES // channels
    pad = wst.shape[2] // 2
    rows_out = length // (n_head * n_sub)
    blocks_out = rows_out // BLOCK
    s = lax.axis_index("seq")
    x = lax.axis_index("head")
    u = lax.axis_index("hsub")

    barrier = pltpu.get_barrier_semaphore()

    @pl.when(s > 0)
    def _():
        pl.semaphore_signal(barrier, inc=1, device_id={"seq": s - 1}, device_id_type=MESH)

    @pl.when(s < n_seq - 1)
    def _():
        pl.semaphore_signal(barrier, inc=1, device_id={"seq": s + 1}, device_id_type=MESH)

    for e in range(1, n_sub):
        pl.semaphore_signal(
            barrier, inc=1, device_id={"hsub": lax.rem(u + e, n_sub)}, device_id_type=MESH
        )
    for d in range(1, n_head):
        pl.semaphore_signal(
            barrier, inc=1, device_id={"head": lax.rem(x + d, n_head)}, device_id_type=MESH
        )

    def rows_of(c):
        return pl.ds(pl.multiple_of(c * BLOCK, BLOCK), BLOCK)

    row_at = lax.broadcasted_iota(jnp.int32, (BLOCK, BLOCK), 0)
    col_at = lax.broadcasted_iota(jnp.int32, (BLOCK, BLOCK), 1)
    upper = row_at <= col_at
    tri = jnp.where(upper, 1.0, 0.0).astype(WIDE)
    e_row = lax.broadcasted_iota(jnp.int32, (2 * pad, cols), 0)
    e_col = lax.broadcasted_iota(jnp.int32, (2 * pad, cols), 1)
    spread = jnp.where(lax.rem(e_row, pad) == e_col // channels, 1.0, 0.0).astype(LOW)
    lane_head = lax.broadcasted_iota(jnp.int32, (BLOCK, LANES), 1) // channels

    if heads < pad:
        wst[...] = jnp.zeros_like(wst)
    own_f[...] = jnp.zeros_like(own_f)
    own_b[...] = jnp.zeros_like(own_b)
    total[...] = jnp.ones_like(total)
    for c in range(count):
        stacked[c * heads:(c + 1) * heads, :] = ld_ref[:, c * BLOCK:(c + 1) * BLOCK]
    sums = lax.dot_general(
        stacked[...], tri, (((1,), (0,)), ((), ())),
        precision=lax.Precision.HIGHEST, preferred_element_type=WIDE,
    )
    for slot, w in enumerate((jnp.exp(sums - sums[:, BLOCK - 1:BLOCK]), jnp.exp(-sums))):
        high = w.astype(LOW).astype(WIDE)
        rest = w - high
        for c in range(count):
            wst[c, slot, 0:heads, :] = high[c * heads:(c + 1) * heads, :]
            wst[c, slot, pad:pad + heads, :] = rest[c * heads:(c + 1) * heads, :]
    for c in range(count):
        within[c] = sums[c * heads:(c + 1) * heads, :]

    def block_sums(t, _):
        blocks = [t * DEEP + r for r in range(DEEP)]
        rows = [rows_of(c) for c in blocks]
        tails = [product(wst[c, 0].astype(LOW), spread, (0, 0)) for c in blocks]
        leads = [product(wst[c, 1].astype(LOW), spread, (0, 0)) for c in blocks]
        vs = [(w * v_ref[r, :].astype(WIDE)).astype(LOW) for w, r in zip(tails, rows)]
        gs = [(w * g_ref[r, :].astype(WIDE)).astype(LOW) for w, r in zip(leads, rows)]
        bs = [product(k_ref[r, :], scaled, (0, 0)) for scaled, r in zip(vs, rows)]
        a_s = [product(q_ref[r, :], scaled, (0, 0)) for scaled, r in zip(gs, rows)]
        for k in range(chunks):
            part = slice(k * LANES, (k + 1) * LANES)
            f, b, whole = own_f[k], own_b[k], total[k]
            for r in range(DEEP):
                decay = leads[r][BLOCK - 1:BLOCK, part]
                decays[blocks[r], k] = decay
                f = decay * f + bs[r][:, part]
                b = b + whole * a_s[r][:, part]
                whole = whole * decay
            own_f[k] = f
            own_b[k] = b
            total[k] = whole
        for r in range(DEEP):
            tw[rows[r], :] = tails[r]
            tv[rows[r], :] = vs[r]
            lg[rows[r], :] = gs[r]
            states[blocks[r]] = bs[r]
            adjoints[blocks[r]] = a_s[r]
        return 0

    lax.fori_loop(0, count // DEEP, block_sums, 0)

    def f_copy(k):
        return pltpu.make_async_remote_copy(
            src_ref=f_out.at[k], dst_ref=f_in.at[k], send_sem=f_send.at[k], recv_sem=f_recv.at[k],
            device_id={"seq": lax.rem(s + 1, n_seq)}, device_id_type=MESH,
        )

    def b_copy(k):
        return pltpu.make_async_remote_copy(
            src_ref=b_out.at[k], dst_ref=b_in.at[k], send_sem=b_send.at[k], recv_sem=b_recv.at[k],
            device_id={"seq": lax.rem(s + n_seq - 1, n_seq)}, device_id_type=MESH,
        )

    near = jnp.where(s > 0, 1, 0) + jnp.where(s < n_seq - 1, 1, 0) + (n_sub - 1) + (n_head - 1)
    pl.semaphore_wait(barrier, near)

    @pl.when(s == 0)
    def _():
        f_in[...] = jnp.zeros_like(f_in)

    @pl.when(s == n_seq - 1)
    def _():
        b_in[...] = jnp.zeros_like(b_in)

    if n_seq > 1:
        @pl.when(s == 0)
        def _():
            for k in range(chunks):
                f_out[k] = own_f[k]
                f_copy(k).start()

        @pl.when(s == n_seq - 1)
        def _():
            for k in range(chunks):
                b_out[k] = own_b[k]
                b_copy(k).start()

    turns = count // UNROLL
    f_at = jnp.minimum(3 * s - 2, turns - chunks)
    b_at = jnp.minimum(3 * (n_seq - 1 - s) - 2, turns - chunks)

    def mask(wt, wt_t, h):
        return jnp.exp(jnp.minimum(wt_t[:, h:h + 1] - wt[h:h + 1, :], 0.0))

    def pair_rows(c):
        rows = rows_of(c)
        wt = within[c]
        wt_t = wt.T
        pair_sum = jnp.zeros((BLOCK, BLOCK), WIDE)
        for p in range(chunks):
            part = slice(p * LANES, (p + 1) * LANES)
            v2 = v_ref[rows, part]
            g2 = g_ref[rows, part]
            stack = jnp.concatenate(
                [jnp.where(lane_head == r, v2, jnp.zeros_like(v2)) for r in range(per)], axis=0
            )
            pairs = product(stack, g2, (1, 1))
            for r in range(per):
                pair_sum += mask(wt, wt_t, p * per + r) * pairs[r * BLOCK:(r + 1) * BLOCK, :]
        pair_low = jnp.where(upper, pair_sum, 0.0).astype(LOW)
        return product(pair_low, k_ref[rows, :], (0, 0)), product(pair_low, q_ref[rows, :], (1, 0))

    def pair_work(c, _):
        found = [pair_rows(c * UNROLL + r) for r in range(UNROLL)]
        for r in range(UNROLL):
            for which in range(2):
                acc[which, rows_of(c * UNROLL + r), :] = found[r][which]

        if n_seq > 1:
            kf = c - f_at

            @pl.when((s > 0) & (s < n_seq - 1) & (kf >= 0) & (kf < chunks))
            def _():
                f_copy(kf).wait_recv()
                f_out[kf] = total[kf] * f_in[kf] + own_f[kf]
                f_copy(kf).start()

            kb = c - b_at

            @pl.when((s > 0) & (s < n_seq - 1) & (kb >= 0) & (kb < chunks))
            def _():
                b_copy(kb).wait_recv()
                b_out[kb] = total[kb] * b_in[kb] + own_b[kb]
                b_copy(kb).start()
        return 0

    lax.fori_loop(0, count // UNROLL, pair_work, 0)

    if n_seq > 1:
        @pl.when(s == n_seq - 1)
        def _():
            for k in range(chunks):
                f_copy(k).wait_recv()

        @pl.when(s == 0)
        def _():
            for k in range(chunks):
                b_copy(k).wait_recv()

    for k in range(chunks):
        part = slice(k * LANES, (k + 1) * LANES)

        def step(c, carry, k=k, part=part):
            f, b = carry
            e = count - 1 - c
            ent[c, :, part] = f.astype(LOW)
            aft[e, :, part] = b.astype(LOW)
            return (decays[c, k] * f + states[c, :, part], decays[e, k] * b + adjoints[e, :, part])

        lax.fori_loop(0, count, step, (f_in[k], b_in[k]))

    def carried(which, base):
        left, right = ((lg, ent), (tv, aft))[which]
        rows = [rows_of(base * blocks_out + r) for r in range(blocks_out)]
        found = [
            acc[which, rows[r], :] + product(left[rows[r], :], right[base * blocks_out + r], (1, 1))
            for r in range(blocks_out)
        ]
        for r in range(blocks_out):
            acc[which, rows[r], :] = found[r]

    def piece(base):
        return pl.ds(pl.multiple_of(base * rows_out, rows_out), rows_out)

    def a_copy(d, e, which):
        far = lax.rem(u + e, n_sub)
        base = lax.rem(x + d, n_head) * n_sub + far
        return pltpu.make_async_remote_copy(
            src_ref=acc.at[which, piece(base)], dst_ref=buf_a.at[d, e - 1, which],
            send_sem=a_send.at[d, e - 1, which], recv_sem=a_recv.at[d, e - 1, which],
            device_id={"hsub": far}, device_id_type=MESH,
        )

    def x_copy(d, which):
        far = lax.rem(x + d, n_head)
        return pltpu.make_async_remote_copy(
            src_ref=acc.at[which, piece(far * n_sub + u)], dst_ref=buf_b.at[d - 1, which],
            send_sem=x_send.at[d - 1, which], recv_sem=x_recv.at[d - 1, which],
            device_id={"head": far}, device_id_type=MESH,
        )

    order = list(range(1, n_head)) + [0]
    for d in order:
        far = lax.rem(x + d, n_head)
        for which in range(2):
            for e in range(1, n_sub):
                carried(which, far * n_sub + lax.rem(u + e, n_sub))
                a_copy(d, e, which).start()
        for which in range(2):
            carried(which, far * n_sub + u)
        for which in range(2):
            own = piece(far * n_sub + u)
            for e in range(1, n_sub):
                a_copy(d, e, which).wait_recv()
                acc[which, own, :] += buf_a[d, e - 1, which]
            if d > 0:
                x_copy(d, which).start()

    def value_rows(c):
        rows = rows_of(c)
        wt = within[c]
        wt_t = wt.T
        key = k_ref[rows, :]
        scores = jnp.where(upper, product(key, q_ref[rows, :], (1, 1)), 0.0)
        back = product(key, aft[c], (1, 0)) * tw[rows, :]
        found = []
        for p in range(chunks):
            part = slice(p * LANES, (p + 1) * LANES)
            g2 = g_ref[rows, part]
            mixed = jnp.concatenate(
                [(mask(wt, wt_t, p * per + r) * scores).astype(LOW) for r in range(per)], axis=1
            )
            stack = jnp.concatenate(
                [jnp.where(lane_head == r, g2, jnp.zeros_like(g2)) for r in range(per)], axis=0
            )
            found.append((product(mixed, stack, (1, 0)) + back[:, part]).astype(LOW))
        return found

    def value_work(c, _):
        found = [value_rows(c * DEEP + r) for r in range(DEEP)]
        for r in range(DEEP):
            for p in range(chunks):
                val_ref[rows_of(c * DEEP + r), p * LANES:(p + 1) * LANES] = found[r][p]
        return 0

    lax.fori_loop(0, count // DEEP, value_work, 0)

    mine = piece(x * n_sub + u)
    for which, out in ((0, qg_ref), (1, kg_ref)):
        result = acc[which, mine, :]
        for d in range(1, n_head):
            x_copy(d, which).wait_recv()
            result = result + buf_b[d - 1, which]
        out[...] = result

    for which in range(2):
        for d in range(n_head):
            for e in range(1, n_sub):
                a_copy(d, e, which).wait_send()
        for d in range(1, n_head):
            x_copy(d, which).wait_send()

    @pl.when(s < n_seq - 1)
    def _():
        for k in range(chunks):
            f_copy(k).wait_send()

    @pl.when(s > 0)
    def _():
        for k in range(chunks):
            b_copy(k).wait_send()


def local(sizes, token_values, key_proj, query_proj, log_decay, out_grad):
    n_seq, n_head, n_sub = sizes
    length, cols = token_values.shape
    heads = log_decay.shape[0]
    state = key_proj.shape[1]
    count = length // BLOCK
    chunks = cols // LANES
    pad = (heads + 7) // 8 * 8
    rows_out = length // (n_head * n_sub)
    vmem = pl.BlockSpec(memory_space=pltpu.VMEM)
    dma = pltpu.SemaphoreType.DMA
    subs = max(n_sub - 1, 1)
    fars = max(n_head - 1, 1)
    square = pltpu.VMEM((chunks, state, LANES), WIDE)
    value_grad, key_grad, query_grad = pl.pallas_call(
        functools.partial(kernel, sizes, heads),
        out_shape=(
            pltpu.VMEM((length, cols), LOW),
            pltpu.VMEM((rows_out, state), WIDE),
            pltpu.VMEM((rows_out, state), WIDE),
        ),
        in_specs=[vmem] * 5,
        out_specs=(vmem, vmem, vmem),
        scratch_shapes=[
            pltpu.VMEM((count, heads, BLOCK), WIDE),
            pltpu.VMEM((count, 2, 2 * pad, BLOCK), WIDE),
            pltpu.VMEM((count * heads, BLOCK), WIDE),
            pltpu.VMEM((length, cols), LOW),
            pltpu.VMEM((length, cols), LOW),
            pltpu.VMEM((length, cols), WIDE),
            pltpu.VMEM((count, state, cols), WIDE),
            pltpu.VMEM((count, state, cols), WIDE),
            pltpu.VMEM((count, chunks, 1, LANES), WIDE),
            pltpu.VMEM((count, state, cols), LOW),
            pltpu.VMEM((count, state, cols), LOW),
            square, square, pltpu.VMEM((chunks, 1, LANES), WIDE),
            square, square, square, square,
            pltpu.VMEM((2, length, state), WIDE),
            pltpu.VMEM((n_head, subs, 2, rows_out, state), WIDE),
            pltpu.VMEM((fars, 2, rows_out, state), WIDE),
            dma((chunks,)), dma((chunks,)), dma((chunks,)), dma((chunks,)),
            dma((n_head, subs, 2)), dma((n_head, subs, 2)),
            dma((fars, 2)), dma((fars, 2)),
        ],
        compiler_params=pltpu.CompilerParams(
            collective_id=0, has_side_effects=True, vmem_limit_bytes=56 * 1024 * 1024
        ),
    )(token_values, key_proj, query_proj, log_decay, out_grad)
    return value_grad, key_grad, query_grad


def solution(mesh):
    sizes = (mesh.shape["seq"], mesh.shape["head"], mesh.shape["hsub"])
    placed = (
        P(("groups", "seq"), ("head", "hsub")),
        P(("groups", "seq"), None),
        P(("groups", "seq"), None),
        P(("head", "hsub"), ("groups", "seq")),
        P(("groups", "seq"), ("head", "hsub")),
    )
    return jax.shard_map(
        functools.partial(local, sizes),
        mesh=mesh,
        in_specs=placed,
        out_specs=(
            P(("groups", "seq"), ("head", "hsub")),
            P(("groups", "seq", "head", "hsub"), None),
            P(("groups", "seq", "head", "hsub"), None),
        ),
        check_vma=False,
    )
```

```python
import functools
import jax
import jax.numpy as jnp
from jax import lax
from jax.experimental import pallas as pl
from jax.experimental.pallas import tpu as pltpu
from jax.sharding import PartitionSpec as P

BLOCK = 128
LANES = 128
WIDE = jnp.float32
LOW = jnp.bfloat16
MESH = pl.DeviceIdType.MESH
UNROLL = 2
DEEP = 4


def product(a, b, over):
    return lax.dot_general(a, b, (((over[0],), (over[1],)), ((), ())), preferred_element_type=WIDE)


def kernel(
    sizes, heads,
    v_ref, k_ref, q_ref, ld_ref, g_ref,
    val_ref, kg_ref, qg_ref,
    within, wst, stacked, tv, lg, tw, states, adjoints, decays, ent, aft,
    own_f, own_b, total, f_in, f_out, b_in, b_out, acc, buf_a, buf_b,
    f_send, f_recv, b_send, b_recv, a_send, a_recv, x_send, x_recv,
):
    n_seq, n_head, n_sub = sizes
    length, cols = v_ref.shape
    state = k_ref.shape[1]
    channels = cols // heads
    count = length // BLOCK
    chunks = cols // LANES
    per = LANES // channels
    pad = wst.shape[2] // 2
    rows_out = length // (n_head * n_sub)
    blocks_out = rows_out // BLOCK
    s = lax.axis_index("seq")
    x = lax.axis_index("head")
    u = lax.axis_index("hsub")

    barrier = pltpu.get_barrier_semaphore()

    @pl.when(s > 0)
    def _():
        pl.semaphore_signal(barrier, inc=1, device_id={"seq": s - 1}, device_id_type=MESH)

    @pl.when(s < n_seq - 1)
    def _():
        pl.semaphore_signal(barrier, inc=1, device_id={"seq": s + 1}, device_id_type=MESH)

    for e in range(1, n_sub):
        pl.semaphore_signal(
            barrier, inc=1, device_id={"hsub": lax.rem(u + e, n_sub)}, device_id_type=MESH
        )
    for d in range(1, n_head):
        pl.semaphore_signal(
            barrier, inc=1, device_id={"head": lax.rem(x + d, n_head)}, device_id_type=MESH
        )

    def rows_of(c):
        return pl.ds(pl.multiple_of(c * BLOCK, BLOCK), BLOCK)

    row_at = lax.broadcasted_iota(jnp.int32, (BLOCK, BLOCK), 0)
    col_at = lax.broadcasted_iota(jnp.int32, (BLOCK, BLOCK), 1)
    upper = row_at <= col_at
    tri = jnp.where(upper, 1.0, 0.0).astype(WIDE)
    e_row = lax.broadcasted_iota(jnp.int32, (2 * pad, cols), 0)
    e_col = lax.broadcasted_iota(jnp.int32, (2 * pad, cols), 1)
    spread = jnp.where(lax.rem(e_row, pad) == e_col // channels, 1.0, 0.0).astype(LOW)
    lane_head = lax.broadcasted_iota(jnp.int32, (BLOCK, LANES), 1) // channels

    if heads < pad:
        wst[...] = jnp.zeros_like(wst)
    own_f[...] = jnp.zeros_like(own_f)
    own_b[...] = jnp.zeros_like(own_b)
    total[...] = jnp.ones_like(total)
    for c in range(count):
        stacked[c * heads:(c + 1) * heads, :] = ld_ref[:, c * BLOCK:(c + 1) * BLOCK]
    sums = lax.dot_general(
        stacked[...], tri, (((1,), (0,)), ((), ())),
        precision=lax.Precision.HIGHEST, preferred_element_type=WIDE,
    )
    for slot, w in enumerate((jnp.exp(sums - sums[:, BLOCK - 1:BLOCK]), jnp.exp(-sums))):
        high = w.astype(LOW).astype(WIDE)
        rest = w - high
        for c in range(count):
            wst[c, slot, 0:heads, :] = high[c * heads:(c + 1) * heads, :]
            wst[c, slot, pad:pad + heads, :] = rest[c * heads:(c + 1) * heads, :]
    for c in range(count):
        within[c] = sums[c * heads:(c + 1) * heads, :]

    def block_sums(t, _):
        blocks = [t * DEEP + r for r in range(DEEP)]
        rows = [rows_of(c) for c in blocks]
        tails = [product(wst[c, 0].astype(LOW), spread, (0, 0)) for c in blocks]
        leads = [product(wst[c, 1].astype(LOW), spread, (0, 0)) for c in blocks]
        vs = [(w * v_ref[r, :].astype(WIDE)).astype(LOW) for w, r in zip(tails, rows)]
        gs = [(w * g_ref[r, :].astype(WIDE)).astype(LOW) for w, r in zip(leads, rows)]
        bs = [product(k_ref[r, :], scaled, (0, 0)) for scaled, r in zip(vs, rows)]
        a_s = [product(q_ref[r, :], scaled, (0, 0)) for scaled, r in zip(gs, rows)]
        for k in range(chunks):
            part = slice(k * LANES, (k + 1) * LANES)
            f, b, whole = own_f[k], own_b[k], total[k]
            for r in range(DEEP):
                decay = leads[r][BLOCK - 1:BLOCK, part]
                decays[blocks[r], k] = decay
                f = decay * f + bs[r][:, part]
                b = b + whole * a_s[r][:, part]
                whole = whole * decay
            own_f[k] = f
            own_b[k] = b
            total[k] = whole
        for r in range(DEEP):
            tw[rows[r], :] = tails[r]
            tv[rows[r], :] = vs[r]
            lg[rows[r], :] = gs[r]
            states[blocks[r]] = bs[r]
            adjoints[blocks[r]] = a_s[r]
        return 0

    lax.fori_loop(0, count // DEEP, block_sums, 0)

    def f_copy(k):
        return pltpu.make_async_remote_copy(
            src_ref=f_out.at[k], dst_ref=f_in.at[k], send_sem=f_send.at[k], recv_sem=f_recv.at[k],
            device_id={"seq": lax.rem(s + 1, n_seq)}, device_id_type=MESH,
        )

    def b_copy(k):
        return pltpu.make_async_remote_copy(
            src_ref=b_out.at[k], dst_ref=b_in.at[k], send_sem=b_send.at[k], recv_sem=b_recv.at[k],
            device_id={"seq": lax.rem(s + n_seq - 1, n_seq)}, device_id_type=MESH,
        )

    near = jnp.where(s > 0, 1, 0) + jnp.where(s < n_seq - 1, 1, 0) + (n_sub - 1) + (n_head - 1)
    pl.semaphore_wait(barrier, near)

    @pl.when(s == 0)
    def _():
        f_in[...] = jnp.zeros_like(f_in)

    @pl.when(s == n_seq - 1)
    def _():
        b_in[...] = jnp.zeros_like(b_in)

    if n_seq > 1:
        @pl.when(s == 0)
        def _():
            for k in range(chunks):
                f_out[k] = own_f[k]
                f_copy(k).start()

        @pl.when(s == n_seq - 1)
        def _():
            for k in range(chunks):
                b_out[k] = own_b[k]
                b_copy(k).start()

    turns = count // UNROLL
    f_at = jnp.minimum(3 * s - 2, turns - chunks)
    b_at = jnp.minimum(3 * (n_seq - 1 - s) - 2, turns - chunks)

    def mask(wt, wt_t, h):
        return jnp.exp(jnp.minimum(wt_t[:, h:h + 1] - wt[h:h + 1, :], 0.0))

    def pair_rows(c):
        rows = rows_of(c)
        wt = within[c]
        wt_t = wt.T
        pair_sum = jnp.zeros((BLOCK, BLOCK), WIDE)
        for p in range(chunks):
            part = slice(p * LANES, (p + 1) * LANES)
            v2 = v_ref[rows, part]
            g2 = g_ref[rows, part]
            stack = jnp.concatenate(
                [jnp.where(lane_head == r, v2, jnp.zeros_like(v2)) for r in range(per)], axis=0
            )
            pairs = product(stack, g2, (1, 1))
            for r in range(per):
                pair_sum += mask(wt, wt_t, p * per + r) * pairs[r * BLOCK:(r + 1) * BLOCK, :]
        pair_low = jnp.where(upper, pair_sum, 0.0).astype(LOW)
        return product(pair_low, k_ref[rows, :], (0, 0)), product(pair_low, q_ref[rows, :], (1, 0))

    def pair_work(c, _):
        found = [pair_rows(c * UNROLL + r) for r in range(UNROLL)]
        for r in range(UNROLL):
            for which in range(2):
                acc[which, rows_of(c * UNROLL + r), :] = found[r][which]

        if n_seq > 1:
            kf = c - f_at

            @pl.when((s > 0) & (s < n_seq - 1) & (kf >= 0) & (kf < chunks))
            def _():
                f_copy(kf).wait_recv()
                f_out[kf] = total[kf] * f_in[kf] + own_f[kf]
                f_copy(kf).start()

            kb = c - b_at

            @pl.when((s > 0) & (s < n_seq - 1) & (kb >= 0) & (kb < chunks))
            def _():
                b_copy(kb).wait_recv()
                b_out[kb] = total[kb] * b_in[kb] + own_b[kb]
                b_copy(kb).start()
        return 0

    lax.fori_loop(0, count // UNROLL, pair_work, 0)

    if n_seq > 1:
        @pl.when(s == n_seq - 1)
        def _():
            for k in range(chunks):
                f_copy(k).wait_recv()

        @pl.when(s == 0)
        def _():
            for k in range(chunks):
                b_copy(k).wait_recv()

    for k in range(chunks):
        part = slice(k * LANES, (k + 1) * LANES)

        def step(c, carry, k=k, part=part):
            f, b = carry
            e = count - 1 - c
            ent[c, :, part] = f.astype(LOW)
            aft[e, :, part] = b.astype(LOW)
            return (decays[c, k] * f + states[c, :, part], decays[e, k] * b + adjoints[e, :, part])

        lax.fori_loop(0, count, step, (f_in[k], b_in[k]))

    def carried(which, base):
        left, right = ((lg, ent), (tv, aft))[which]
        rows = [rows_of(base * blocks_out + r) for r in range(blocks_out)]
        found = [
            acc[which, rows[r], :] + product(left[rows[r], :], right[base * blocks_out + r], (1, 1))
            for r in range(blocks_out)
        ]
        for r in range(blocks_out):
            acc[which, rows[r], :] = found[r]

    def piece(base):
        return pl.ds(pl.multiple_of(base * rows_out, rows_out), rows_out)

    def a_copy(d, e, which):
        far = lax.rem(u + e, n_sub)
        base = lax.rem(x + d, n_head) * n_sub + far
        return pltpu.make_async_remote_copy(
            src_ref=acc.at[which, piece(base)], dst_ref=buf_a.at[d, e - 1, which],
            send_sem=a_send.at[d, e - 1, which], recv_sem=a_recv.at[d, e - 1, which],
            device_id={"hsub": far}, device_id_type=MESH,
        )

    def x_copy(d, which):
        far = lax.rem(x + d, n_head)
        return pltpu.make_async_remote_copy(
            src_ref=acc.at[which, piece(far * n_sub + u)], dst_ref=buf_b.at[d - 1, which],
            send_sem=x_send.at[d - 1, which], recv_sem=x_recv.at[d - 1, which],
            device_id={"head": far}, device_id_type=MESH,
        )

    order = list(range(1, n_head)) + [0]
    for d in order:
        far = lax.rem(x + d, n_head)
        for which in range(2):
            for e in range(1, n_sub):
                carried(which, far * n_sub + lax.rem(u + e, n_sub))
                a_copy(d, e, which).start()
        for which in range(2):
            carried(which, far * n_sub + u)
            own = piece(far * n_sub + u)
            for e in range(1, n_sub):
                a_copy(d, e, which).wait_recv()
                acc[which, own, :] += buf_a[d, e - 1, which]
            if d > 0:
                x_copy(d, which).start()

    def value_rows(c):
        rows = rows_of(c)
        wt = within[c]
        wt_t = wt.T
        key = k_ref[rows, :]
        scores = jnp.where(upper, product(key, q_ref[rows, :], (1, 1)), 0.0)
        back = product(key, aft[c], (1, 0)) * tw[rows, :]
        found = []
        for p in range(chunks):
            part = slice(p * LANES, (p + 1) * LANES)
            g2 = g_ref[rows, part]
            mixed = jnp.concatenate(
                [(mask(wt, wt_t, p * per + r) * scores).astype(LOW) for r in range(per)], axis=1
            )
            stack = jnp.concatenate(
                [jnp.where(lane_head == r, g2, jnp.zeros_like(g2)) for r in range(per)], axis=0
            )
            found.append((product(mixed, stack, (1, 0)) + back[:, part]).astype(LOW))
        return found

    def value_work(c, _):
        found = [value_rows(c * DEEP + r) for r in range(DEEP)]
        for r in range(DEEP):
            for p in range(chunks):
                val_ref[rows_of(c * DEEP + r), p * LANES:(p + 1) * LANES] = found[r][p]
        return 0

    lax.fori_loop(0, count // DEEP, value_work, 0)

    mine = piece(x * n_sub + u)
    for which, out in ((0, qg_ref), (1, kg_ref)):
        result = acc[which, mine, :]
        for d in range(1, n_head):
            x_copy(d, which).wait_recv()
            result = result + buf_b[d - 1, which]
        out[...] = result

    for which in range(2):
        for d in range(n_head):
            for e in range(1, n_sub):
                a_copy(d, e, which).wait_send()
        for d in range(1, n_head):
            x_copy(d, which).wait_send()

    @pl.when(s < n_seq - 1)
    def _():
        for k in range(chunks):
            f_copy(k).wait_send()

    @pl.when(s > 0)
    def _():
        for k in range(chunks):
            b_copy(k).wait_send()


def local(sizes, token_values, key_proj, query_proj, log_decay, out_grad):
    n_seq, n_head, n_sub = sizes
    length, cols = token_values.shape
    heads = log_decay.shape[0]
    state = key_proj.shape[1]
    count = length // BLOCK
    chunks = cols // LANES
    pad = (heads + 7) // 8 * 8
    rows_out = length // (n_head * n_sub)
    vmem = pl.BlockSpec(memory_space=pltpu.VMEM)
    dma = pltpu.SemaphoreType.DMA
    subs = max(n_sub - 1, 1)
    fars = max(n_head - 1, 1)
    square = pltpu.VMEM((chunks, state, LANES), WIDE)
    value_grad, key_grad, query_grad = pl.pallas_call(
        functools.partial(kernel, sizes, heads),
        out_shape=(
            pltpu.VMEM((length, cols), LOW),
            pltpu.VMEM((rows_out, state), WIDE),
            pltpu.VMEM((rows_out, state), WIDE),
        ),
        in_specs=[vmem] * 5,
        out_specs=(vmem, vmem, vmem),
        scratch_shapes=[
            pltpu.VMEM((count, heads, BLOCK), WIDE),
            pltpu.VMEM((count, 2, 2 * pad, BLOCK), WIDE),
            pltpu.VMEM((count * heads, BLOCK), WIDE),
            pltpu.VMEM((length, cols), LOW),
            pltpu.VMEM((length, cols), LOW),
            pltpu.VMEM((length, cols), WIDE),
            pltpu.VMEM((count, state, cols), WIDE),
            pltpu.VMEM((count, state, cols), WIDE),
            pltpu.VMEM((count, chunks, 1, LANES), WIDE),
            pltpu.VMEM((count, state, cols), LOW),
            pltpu.VMEM((count, state, cols), LOW),
            square, square, pltpu.VMEM((chunks, 1, LANES), WIDE),
            square, square, square, square,
            pltpu.VMEM((2, length, state), WIDE),
            pltpu.VMEM((n_head, subs, 2, rows_out, state), WIDE),
            pltpu.VMEM((fars, 2, rows_out, state), WIDE),
            dma((chunks,)), dma((chunks,)), dma((chunks,)), dma((chunks,)),
            dma((n_head, subs, 2)), dma((n_head, subs, 2)),
            dma((fars, 2)), dma((fars, 2)),
        ],
        compiler_params=pltpu.CompilerParams(
            collective_id=0, has_side_effects=True, vmem_limit_bytes=56 * 1024 * 1024
        ),
    )(token_values, key_proj, query_proj, log_decay, out_grad)
    return value_grad, key_grad, query_grad


def solution(mesh):
    sizes = (mesh.shape["seq"], mesh.shape["head"], mesh.shape["hsub"])
    placed = (
        P(("groups", "seq"), ("head", "hsub")),
        P(("groups", "seq"), None),
        P(("groups", "seq"), None),
        P(("head", "hsub"), ("groups", "seq")),
        P(("groups", "seq"), ("head", "hsub")),
    )
    return jax.shard_map(
        functools.partial(local, sizes),
        mesh=mesh,
        in_specs=placed,
        out_specs=(
            P(("groups", "seq"), ("head", "hsub")),
            P(("groups", "seq", "head", "hsub"), None),
            P(("groups", "seq", "head", "hsub"), None),
        ),
        check_vma=False,
    )
```
